512 devices in a mesh: ctx: 32 (over x, z), batch: 16 (over y, core).
Axes of the slice: x: 4, y: 8, z: 8, core: 2. Of those that a mesh axis runs over, the one named last changes fastest.
Arguments:
- latent_cache: bfloat16 [32, 32768, 576], P('batch', 'ctx'), may hold values from -6 to 6
- queries: bfloat16 [8, 32, 128, 576], P(None, 'batch', 'ctx'), may hold values from -72 to 72
- new_latent: bfloat16 [8, 32, 576], P(None, 'batch'), may hold values from -9 to 9
- lengths: int32 [32], P('batch'), may hold values from 4096 to 32768, as said below
- selection: int32 [8, 32, 32], P(None, 'batch'), may hold values from 0 to 511, as said below
- w_uv: bfloat16 [128, 512, 128], P('ctx'), may hold values from -0.5 to 0.5
- w_out: bfloat16 [16384, 7168], P('ctx', 'batch'), may hold values from -0.1875 to 0.1875
Outputs:
- attention_out: bfloat16 [256, 7168], P('ctx', 'batch')
The draws below stay inside these ranges and needn't reach their ends.
Inputs may be any that keep to these rules, and one draw needn't show every extreme that they name: `lengths`: every row holds at least 4096 positions; one row holds exactly that many and another exactly 32768. `selection`: for each step and row, 32 distinct block numbers in ascending order, each block starting below the row's length. At most 8 of them fall in one context shard (an aligned run of 16 blocks), and some row of every draw has exactly 8 in a shard.
All inputs are finite; a program needn't handle non-finite values.
Results may differ from the reference program's by a relative error of at most 0.022.
Values may be sent and summed in bfloat16 or wider, within the bound.
No kernel may reach another device: no remote copies, remote signals or barrier semaphores. Data moves between devices by JAX's collectives and lax.ppermute only.
A program may use at most 128 MiB of HBM per device.

```python
import jax
import jax.numpy as jnp
from jax import lax

HEADS = 128
LATENT = 512
ROPE = 64
HEAD_DIM = 128
D_MODEL = 7168
BLOCK = 64
TOPK = 32
KMAX = 8
STEPS = 8
CTX_DEV = 1024
QK_DIM = 576
ROWS = 32
CONTEXT = 32768


def new_keys(key, tie_weight):
    base_draw = 1.5 * jnp.clip(jax.random.normal(jax.random.fold_in(key, 101), (STEPS, ROWS, QK_DIM), jnp.float32), -6.0, 6.0)
    odd_steps = (jnp.arange(STEPS) % 2 == 1).astype(jnp.float32)[:, None, None]
    blend = odd_steps * tie_weight
    return base_draw * (1.0 - blend)


def context_lengths(key):
    sub_key = jax.random.fold_in(key, 201)
    shortest = TOPK // KMAX * CTX_DEV
    lengths = jax.random.randint(sub_key, (ROWS,), shortest, CONTEXT + 1)
    short_row = jax.random.randint(jax.random.fold_in(sub_key, 1), (), 0, ROWS)
    long_row = (short_row + 1 + jax.random.randint(jax.random.fold_in(sub_key, 2), (), 0, ROWS - 1)) % ROWS
    lengths = lengths.at[short_row].set(shortest)
    lengths = lengths.at[long_row].set(CONTEXT)
    return lengths.astype(jnp.int32)


def draw_latent_cache(key, part):
    key = jax.random.fold_in(key, 11)
    base_draw = jnp.clip(jax.random.normal(key, (ROWS, CONTEXT // BLOCK, BLOCK, QK_DIM), jnp.float32), -6.0, 6.0)
    return base_draw.reshape(ROWS, CONTEXT, QK_DIM).astype(jnp.bfloat16)


def draw_new_latent(key, part):
    tie_weight = 0.0
    return new_keys(key, tie_weight).astype(jnp.bfloat16)


def draw_queries(key, part):
    key = jax.random.fold_in(key, 7)
    base_draw = 1.2 * jnp.clip(jax.random.normal(key, (STEPS, ROWS, HEADS, QK_DIM), jnp.float32), -5.0, 5.0)
    return base_draw.astype(jnp.bfloat16)


def draw_lengths(key, part):
    return context_lengths(key)


def draw_selection(key, part):
    lengths = context_lengths(key)
    key = jax.random.fold_in(key, 301)
    block_count = CONTEXT // BLOCK
    shard_blocks = CTX_DEV // BLOCK
    block_ids = jnp.arange(block_count, dtype=jnp.int32)
    valid_mask = (block_ids[None, :] * BLOCK < lengths[:, None])[None]
    first_rank = jax.random.randint(jax.random.fold_in(key, 1), (STEPS, ROWS, block_count), 0, 2 ** 20) * block_count + block_ids
    first_rank = jnp.where(valid_mask, first_rank, -1 - block_ids)
    grouped = first_rank.reshape(STEPS, ROWS, block_count // shard_blocks, shard_blocks)
    order_inside = jnp.argsort(jnp.argsort(-grouped, axis=3, stable=True), axis=3, stable=True)
    eligible = valid_mask & (order_inside.reshape(STEPS, ROWS, block_count) < KMAX)
    second_rank = jax.random.randint(jax.random.fold_in(key, 2), (STEPS, ROWS, block_count), 0, 2 ** 20) * block_count + block_ids
    second_rank = jnp.where(eligible, second_rank, -1 - block_ids)
    picked = jax.lax.top_k(second_rank, TOPK)[1]
    return jnp.sort(picked, axis=2).astype(jnp.int32)


def shard_levels(rng, dims, pieces, low, largest):
    def one(position, shards_of):
        draws = jax.random.uniform(jax.random.fold_in(jax.random.fold_in(rng, 6), position), (shards_of,), jnp.float32, low / len(pieces), largest / len(pieces))
        return jnp.repeat(jnp.exp(draws), dims[position] // shards_of).reshape((-1,) + (1,) * (len(dims) - position - 1))

    factor_of = one(*pieces[0])
    for cut in pieces[1:]:
        factor_of = factor_of * one(*cut)
    return factor_of


def noise(key, dims, scale, most, pieces=(), held_as=jnp.bfloat16):
    gain = shard_levels(key, dims, pieces, -0.22, 0.18) if pieces else 1.0
    values = jax.random.normal(key, dims, jnp.float32) * scale * gain
    return jnp.minimum(jnp.maximum(values, -most), most).astype(held_as)


def setup_inputs(seed: int = 0) -> dict:
    key_of = jax.random.split(jax.random.key(seed), 8)
    latent_cache = draw_latent_cache(jax.random.fold_in(key_of[7], 71), 0)
    queries = draw_queries(jax.random.fold_in(key_of[7], 71), 0)
    new_latent = draw_new_latent(jax.random.fold_in(key_of[7], 71), 0)
    lengths = draw_lengths(jax.random.fold_in(key_of[7], 71), 0)
    selection = draw_selection(jax.random.fold_in(key_of[7], 71), 0)
    w_uv = noise(key_of[5], (HEADS, LATENT, HEAD_DIM), (LATENT // 4) ** -0.5, 0.5, ((0, 32),))
    w_out = noise(key_of[6], (HEADS * HEAD_DIM, D_MODEL), (HEADS * HEAD_DIM // 16) ** -0.5, 0.1875, ((0, 32), (1, 16)))
    return {"latent_cache": latent_cache, "queries": queries, "new_latent": new_latent, "lengths": lengths, "selection": selection, "w_uv": w_uv, "w_out": w_out}


neg_fill = -1.0e30
score_scale = 192.0 ** -0.5
top_precision = lax.Precision.HIGHEST


def round_half(value):
    return lax.optimization_barrier(value.astype(jnp.bfloat16)).astype(jnp.float32)


def reference(latent_cache, queries, new_latent, lengths, selection, w_uv, w_out):
    shard_blocks = CTX_DEV // BLOCK
    block_count = CONTEXT // BLOCK
    cache_blocks = latent_cache.reshape(ROWS, block_count, BLOCK, LATENT + ROPE)
    offsets = jnp.arange(BLOCK, dtype=jnp.int32)
    slot_order = jnp.arange(TOPK, dtype=jnp.int32)
    step_ids = jnp.arange(STEPS, dtype=jnp.int32)
    up_weights = w_uv.astype(jnp.float32)

    def one_row(flat_index):
        step_index = flat_index // ROWS
        row_index = flat_index % ROWS
        query_rows = queries[step_index, row_index].astype(jnp.float32)
        chosen = selection[step_index, row_index].astype(jnp.int32)
        key_rows = cache_blocks[row_index, chosen].astype(jnp.float32)
        scores = jnp.einsum("hd,kjd->hkj", query_rows, key_rows, precision=top_precision) * score_scale
        live_mask = (chosen[:, None] * BLOCK + offsets[None, :]) < lengths[row_index]
        masked = jnp.where(live_mask[None], scores, neg_fill)
        groups = chosen // shard_blocks
        same_shard = groups[:, None] == groups[None, :]
        block_max = jnp.max(masked, axis=2)
        maxima = jnp.max(jnp.where(same_shard[None], block_max[:, None, :], neg_fill), axis=2)
        maxima = round_half(maxima)
        weights = jnp.where(live_mask[None], jnp.exp(scores - maxima[:, :, None]), 0.0)
        block_totals = jnp.sum(weights, axis=2)
        block_sums = jnp.einsum("hkj,kjl->hkl", round_half(weights), key_rows[:, :, :LATENT], precision=top_precision)
        same_float = same_shard.astype(jnp.float32)
        shard_sums = round_half(jnp.einsum("hkl,km->hml", block_sums, same_float, precision=top_precision))
        shard_totals = round_half(jnp.dot(block_totals, same_float, precision=top_precision))
        earlier = same_shard & (slot_order[None, :] < slot_order[:, None])
        leading = jnp.logical_not(jnp.any(earlier, axis=1))
        fresh_keys = new_latent[:, row_index].astype(jnp.float32)
        own_scores = jnp.dot(query_rows, fresh_keys.T, precision=top_precision) * score_scale
        causal = step_ids <= step_index
        own_max = jnp.max(jnp.where(causal[None], own_scores, neg_fill), axis=1)
        own_weights = jnp.where(causal[None], jnp.exp(own_scores - own_max[:, None]), 0.0)
        own_total = jnp.sum(own_weights, axis=1)
        own_sum = jnp.dot(round_half(own_weights), fresh_keys[:, :LATENT], precision=top_precision)
        overall = jnp.maximum(jnp.max(maxima, axis=1), own_max)
        factor = jnp.where(leading[None], jnp.exp(maxima - overall[:, None]), 0.0)
        own_factor = jnp.exp(own_max - overall)
        numerator = jnp.einsum("hk,hkl->hl", factor, shard_sums, precision=top_precision) + own_factor[:, None] * own_sum
        denominator = jnp.sum(factor * shard_totals, axis=1) + own_factor * own_total
        merged = (numerator / denominator[:, None]).astype(jnp.bfloat16)
        heads_out = jnp.einsum("hl,hlv->hv", merged.astype(jnp.float32), up_weights, precision=top_precision)
        return heads_out.astype(jnp.bfloat16)

    attention = lax.map(one_row, jnp.arange(STEPS * ROWS, dtype=jnp.int32))
    flat_rows = attention.reshape(STEPS * ROWS, HEADS * HEAD_DIM)
    return jnp.dot(flat_rows, w_out, preferred_element_type=jnp.float32).astype(jnp.bfloat16)
```

```python
import functools

import jax
import jax.numpy as jnp
from jax import lax
from jax.experimental import pallas as pl
from jax.experimental.pallas import tpu as pltpu
from jax.sharding import Mesh, PartitionSpec as P

BLOCK = 64
X_SIZE = 4
Z_SIZE = 8
STEPS = 8
LOG2E = 1.4426950408889634
DEAD = -1e30
FLOOR = -1e20
score_scale = 192.0 ** (-0.5)

MIB = 2**20


def params(mib):
    return pltpu.CompilerParams(vmem_limit_bytes=mib * MIB)


def matmul(a, b):
    return jnp.dot(a, b, preferred_element_type=jnp.float32)


def matmul_t(a, b):
    return lax.dot_general(a, b, (((1,), (1,)), ((), ())), preferred_element_type=jnp.float32)


def iota(shape, axis):
    return lax.broadcasted_iota(jnp.int32, shape, axis)


def pack_kernel(q_ref, out_ref):
    count = q_ref.shape[0]
    half = count // 2
    blocks = [q_ref[:, k * 128 : (k + 1) * 128] for k in range(4)]
    rope = q_ref[:, 512:576].astype(jnp.float32)
    wide = jnp.concatenate([rope, rope], axis=1)
    rope = jnp.where(iota((half, 128), 1) < 64, wide[:half], wide[half:]).astype(jnp.bfloat16)
    for z in range(out_ref.shape[0]):
        for k in range(4):
            out_ref[z, k * count : (k + 1) * count, :] = blocks[k]
        out_ref[z, 4 * count :, :] = rope


def pack(q_rows, copies):
    count = q_rows.shape[0]
    return pl.pallas_call(
        pack_kernel,
        out_shape=jax.ShapeDtypeStruct((copies, 4 * count + count // 2, 128), jnp.bfloat16),
        compiler_params=params(8),
        name="pack_queries",
    )(q_rows)


def unpack(refs, r):
    length = refs[0].shape[1]
    count = length * 2 // 9
    half = count // 2
    blocks = []
    for k in range(4):
        at = slice(k * count + r * half, k * count + (r + 1) * half)
        blocks.append(jnp.concatenate([ref[z, at, :] for ref in refs for z in range(ref.shape[0])]))
    latent = jnp.concatenate(blocks, axis=1)
    at = slice(4 * count, 4 * count + half)
    rope = jnp.concatenate([ref[z, at, :] for ref in refs for z in range(ref.shape[0])])
    return latent, rope


def beside(rope, r):
    blank = jnp.zeros_like(rope)
    return jnp.concatenate([rope, blank] if r == 0 else [blank, rope], axis=0)


def partial_kernel(*refs):
    q_refs, (keys_ref, bias_ref, out_ref, cols) = refs[:-4], refs[-4:]
    zs = sum(ref.shape[0] for ref in q_refs)
    chunk = q_refs[0].shape[1] * 2 // 9
    half = chunk // 2
    count = zs * half
    for r in range(2):
        latent, rope = unpack(q_refs, r)
        values = keys_ref[r, :512, :]
        scores = matmul(latent, values) + matmul(rope, beside(keys_ref[r, 512:, :], r))
        bias = bias_ref[r]
        scores = (scores.reshape(count // STEPS, STEPS, -1) + bias[None]).reshape(count, -1)
        top = jnp.maximum(jnp.max(scores, axis=1, keepdims=True) * score_scale, FLOOR)
        top = top.astype(jnp.bfloat16).astype(jnp.float32)
        weights = jnp.exp2(scores * (score_scale * LOG2E) - top * LOG2E)
        total = jnp.sum(weights, axis=1, keepdims=True)
        summed = matmul_t(weights.astype(jnp.bfloat16), values).astype(jnp.bfloat16)
        lanes = iota((count, 128), 1)
        meta = jnp.where(lanes == 0, top, jnp.where(lanes == 1, total, 0.0))
        for z in range(zs):
            at = z * chunk + r * half
            part = slice(z * half, (z + 1) * half)
            out_ref[at : at + half, :] = summed[part]
            cols[at : at + half, :] = meta[part]
    end = zs * chunk
    out_ref[end : end + 16, :] = cols[...].T[:16].astype(jnp.bfloat16)


def local_partial(q_chunks, keys, bias):
    chunk = q_chunks[0].shape[1] * 2 // 9
    queries = sum(q.shape[0] for q in q_chunks) * chunk
    return pl.pallas_call(
        partial_kernel,
        out_shape=jax.ShapeDtypeStruct((queries + 16, 512), jnp.bfloat16),
        scratch_shapes=[pltpu.VMEM((queries, 128), jnp.float32)],
        compiler_params=params(32),
        cost_estimate=pl.CostEstimate(
            flops=2 * queries * keys.shape[2] * 1152,
            bytes_accessed=4 * MIB,
            transcendentals=queries * keys.shape[2],
        ),
        name="local_partial",
    )(*q_chunks, keys, bias)


def combine_kernel(a_ref, b_ref, c_ref, d_ref, out_ref):
    refs = (a_ref, b_ref, c_ref, d_ref)
    zs = out_ref.shape[0]
    chunk = (a_ref.shape[0] - 16) // zs
    count = zs * chunk
    metas = [ref[count : count + 16, :].astype(jnp.float32) for ref in refs]
    tops = [meta[0:1] for meta in metas]
    top = functools.reduce(jnp.maximum, tops)
    factors = [jnp.exp(one - top) for one in tops]
    total = sum(f * meta[1:2] for f, meta in zip(factors, metas))
    place = iota((128, count), 0)
    stacked = jnp.zeros((128, count), jnp.float32)
    for i, f in enumerate(factors):
        stacked = jnp.where(place == i, f, stacked)
    cols = stacked.T
    place = iota((16, count), 0)
    meta = jnp.where(place == 0, top, jnp.where(place == 1, total, 0.0))
    for z in range(zs):
        rows = slice(z * chunk, (z + 1) * chunk)
        merged = sum(
            cols[rows, i : i + 1] * ref[rows, :].astype(jnp.float32) for i, ref in enumerate(refs)
        ).astype(jnp.bfloat16)
        for k in range(4):
            out_ref[z, k * chunk : (k + 1) * chunk, :] = merged[:, k * 128 : (k + 1) * 128]
        tile = meta[:, (z // 2) * 128 : (z // 2 + 1) * 128]
        if z % 2:
            tile = pltpu.roll(tile, 64, 1)
        out_ref[z, 4 * chunk : 4 * chunk + 16, :] = tile.astype(jnp.bfloat16)


def combine(parts, zs, chunk):
    return pl.pallas_call(
        combine_kernel,
        out_shape=jax.ShapeDtypeStruct((zs, 4 * chunk + 16, 128), jnp.bfloat16),
        compiler_params=params(16),
        name="combine_x",
    )(*parts)


def own_kernel(q_ref, fresh_ref, bias_ref, sum_ref, meta_ref):
    half = sum_ref.shape[0] // 2
    for r in range(2):
        latent, rope = unpack([q_ref], r)
        fresh = fresh_ref[r]
        scores = matmul_t(latent, fresh[:, :512])
        wide = jnp.concatenate([fresh[:, 512:].astype(jnp.float32)] * 2, axis=1)
        mine = (iota(wide.shape, 1) < 64) == (r == 0)
        scores = scores + matmul_t(rope, jnp.where(mine, wide, 0.0).astype(jnp.bfloat16))
        scores = (scores.reshape(half // STEPS, STEPS, -1) + bias_ref[...][None]).reshape(half, -1)
        top = jnp.max(scores, axis=1, keepdims=True) * score_scale
        weights = jnp.exp2(scores * (score_scale * LOG2E) - top * LOG2E)
        total = jnp.sum(weights, axis=1, keepdims=True)
        at = slice(r * half, (r + 1) * half)
        sum_ref[at, :] = matmul(weights.astype(jnp.bfloat16), fresh[:, :512])
        lanes = iota((half, 128), 1)
        meta_ref[at, :] = jnp.where(lanes == 0, top, jnp.where(lanes == 1, total, 0.0))


def own_part(packed, fresh, causal):
    length = packed.shape[1]
    count = length * 2 // 9
    return pl.pallas_call(
        own_kernel,
        grid=(1,),
        in_specs=[
            pl.BlockSpec((1, length, 128), lambda i: (0, 0, 0)),
            pl.BlockSpec(fresh.shape, lambda i: (0, 0, 0)),
            pl.BlockSpec(causal.shape, lambda i: (0, 0)),
        ],
        out_specs=[
            pl.BlockSpec((count, 512), lambda i: (0, 0)),
            pl.BlockSpec((count, 128), lambda i: (0, 0)),
        ],
        out_shape=(
            jax.ShapeDtypeStruct((count, 512), jnp.float32),
            jax.ShapeDtypeStruct((count, 128), jnp.float32),
        ),
        compiler_params=params(8),
        name="own_part",
    )(packed, fresh, causal)


def merge_kernel(got_ref, sum_ref, meta_ref, up_ref, out_ref):
    zs = got_ref.shape[0]
    count = sum_ref.shape[0]
    heads = up_ref.shape[0]
    rows = count // (heads * STEPS)
    place = iota((128, 128), 0)
    stacked = jnp.zeros((128, 128), jnp.float32)
    for z in range(zs):
        meta = got_ref[z, 4 * count : 4 * count + 16, :].astype(jnp.float32)
        stacked = jnp.where(place == z, meta[0:1], stacked)
        stacked = jnp.where(place == zs + z, meta[1:2], stacked)
    cols = stacked.T[:count]
    tops, totals = cols[:, :zs], cols[:, zs : 2 * zs]
    own_top, own_total = meta_ref[:, 0:1], meta_ref[:, 1:2]
    top = jnp.maximum(jnp.max(tops, axis=1, keepdims=True), own_top)
    factors = jnp.exp(tops - top)
    own_factor = jnp.exp(own_top - top)
    bottom = jnp.sum(factors * totals, axis=1, keepdims=True) + own_factor * own_total
    pieces = []
    for k in range(4):
        piece = own_factor * sum_ref[:, k * 128 : (k + 1) * 128]
        for z in range(zs):
            block = got_ref[z, k * count : (k + 1) * count, :].astype(jnp.float32)
            piece = piece + factors[:, z : z + 1] * block
        pieces.append(piece / bottom)
    merged = jnp.concatenate(pieces, axis=1)
    for h in range(heads):
        mine = jnp.concatenate(
            [merged[(r * heads + h) * STEPS : (r * heads + h + 1) * STEPS] for r in range(rows)]
        ).astype(jnp.bfloat16)
        lifted = matmul(mine, up_ref[h]).astype(jnp.bfloat16)
        for copy in range(out_ref.shape[0]):
            out_ref[copy, :, h * 128 : (h + 1) * 128] = lifted


def merge(got, own_sum, own_meta, w_uv, copies):
    shape = (copies, own_sum.shape[0] // w_uv.shape[0], w_uv.shape[0] * w_uv.shape[2])
    return pl.pallas_call(
        merge_kernel,
        out_shape=jax.ShapeDtypeStruct(shape, jnp.bfloat16),
        compiler_params=params(16),
        name="merge_up",
    )(got, own_sum, own_meta, w_uv)


def project_kernel(rows_ref, w_ref, out_ref):
    n = rows_ref.shape[0]
    to, come = iota((n, n), 0), iota((n, n), 1)
    rows = n // STEPS
    here = (to % rows) * STEPS + to // rows == come
    here = here.astype(jnp.float32).astype(jnp.bfloat16)
    ordered = matmul(here, rows_ref[...]).astype(jnp.bfloat16)
    out_ref[...] = matmul_t(ordered, w_ref[...]).astype(jnp.bfloat16)


def project(rows, w_out_t):
    return pl.pallas_call(
        project_kernel,
        out_shape=jax.ShapeDtypeStruct((rows.shape[0], w_out_t.shape[0]), jnp.bfloat16),
        compiler_params=params(16),
        name="project_out",
    )(rows, w_out_t)


def shift(value, axis, by, size):
    return lax.ppermute(value, axis, [(i, (i + by) % size) for i in range(size)])


def after(value, earlier):
    return lax.optimization_barrier((value, earlier))[0]


def swap_all(value, axis):
    return lax.all_to_all(value, axis, split_axis=0, concat_axis=0, tiled=True)


def body(latent_cache, queries, new_latent, lengths, selection, w_uv, w_out):
    steps, rows, heads, width = queries.shape
    keys = latent_cache.shape[1]
    shard = lax.axis_index("x") * Z_SIZE + lax.axis_index("z")

    q_rows = jnp.transpose(queries, (1, 2, 0, 3)).reshape(rows * heads * steps, width)
    packed = pack(q_rows, Z_SIZE)
    line = swap_all(packed, "z")
    far = shift(line, "x", 2, X_SIZE)
    left = shift(line, "x", 1, X_SIZE)
    right = shift(line, "x", -1, X_SIZE)

    blocks = shard * (keys // BLOCK) + jnp.arange(keys // BLOCK, dtype=jnp.int32)
    chosen = jnp.any(selection[:, :, :, None] == blocks, axis=2)
    positions = shard * keys + jnp.arange(keys, dtype=jnp.int32)
    live = jnp.repeat(chosen, BLOCK, axis=2) & (positions < lengths[:, None])[None]
    bias = jnp.where(jnp.transpose(live, (1, 0, 2)), 0.0, DEAD)
    cache_t = jnp.transpose(latent_cache, (0, 2, 1))

    ids = jnp.arange(128, dtype=jnp.int32)
    causal = jnp.where(ids[None, :] <= jnp.arange(steps)[:, None], 0.0, DEAD)
    fresh = jnp.pad(jnp.transpose(new_latent, (1, 0, 2)), ((0, 0), (0, 128 - steps), (0, 0)))
    own_sum, own_meta = own_part(packed, fresh, causal)

    here = local_partial([line], cache_t, bias)
    for_left = local_partial([after(left, here)], cache_t, bias)
    for_right = local_partial([right], cache_t, bias)
    for_far = local_partial([far], cache_t, bias)
    parts = [
        here,
        shift(for_left, "x", -1, X_SIZE),
        shift(for_right, "x", 1, X_SIZE),
        shift(for_far, "x", 2, X_SIZE),
    ]
    got = swap_all(combine(parts, Z_SIZE, rows * heads * steps), "z")
    groups = lax.axis_size(("y", "core"))
    attention = swap_all(merge(got, own_sum, own_meta, w_uv, groups), ("y", "core"))
    shares = project(attention.reshape(groups * rows * steps, -1), w_out.T)
    shares = shares.reshape(X_SIZE * Z_SIZE, -1, shares.shape[1])
    got_shares = swap_all(shares, ("x", "z"))
    return jnp.sum(got_shares.astype(jnp.float32), axis=0).astype(jnp.bfloat16)


def solution(mesh):
    batch = mesh.shape["batch"]
    fine = Mesh(mesh.devices.reshape(X_SIZE, Z_SIZE, batch // 2, 2), ("x", "z", "y", "core"))
    ctx, rows = ("x", "z"), ("y", "core")
    return jax.shard_map(
        body,
        mesh=fine,
        in_specs=(
            P(rows, ctx, None),
            P(None, rows, ctx, None),
            P(None, rows, None),
            P(rows),
            P(None, rows, None),
            P(ctx, None, None),
            P(ctx, rows),
        ),
        out_specs=P(ctx, rows),
        check_vma=False,
    )
```

```python
import functools

import jax
import jax.numpy as jnp
from jax import lax
from jax.experimental import pallas as pl
from jax.experimental.pallas import tpu as pltpu
from jax.sharding import Mesh, PartitionSpec as P

BLOCK = 64
X_SIZE = 4
Z_SIZE = 8
STEPS = 8
LOG2E = 1.4426950408889634
DEAD = -1e30
FLOOR = -1e20
score_scale = 192.0 ** (-0.5)

MIB = 2**20


def params(mib):
    return pltpu.CompilerParams(vmem_limit_bytes=mib * MIB)


def matmul(a, b):
    return jnp.dot(a, b, preferred_element_type=jnp.float32)


def matmul_t(a, b):
    return lax.dot_general(a, b, (((1,), (1,)), ((), ())), preferred_element_type=jnp.float32)


def iota(shape, axis):
    return lax.broadcasted_iota(jnp.int32, shape, axis)


PART = 16
FEW, MANY = 5 * PART, 14 * PART


def pack_kernel(q_ref, few_ref, many_ref):
    rope = q_ref[:, 512:576].astype(jnp.float32)
    wide = jnp.concatenate([rope, rope], axis=1)
    low = iota((PART, 128), 1) < 64
    quarter = [wide[i * PART : (i + 1) * PART] for i in range(4)]
    first = jnp.where(low, quarter[0], 0.0).astype(jnp.bfloat16)
    second = jnp.where(low, quarter[1], quarter[2]).astype(jnp.bfloat16)
    third = jnp.where(low, 0.0, quarter[3]).astype(jnp.bfloat16)
    for k in range(4):
        lanes = slice(k * 128, (k + 1) * 128)
        few_ref[k * PART : (k + 1) * PART, :] = q_ref[:PART, lanes]
        for z in range(many_ref.shape[0]):
            many_ref[z, 3 * k * PART : 3 * (k + 1) * PART, :] = q_ref[PART:, lanes]
    few_ref[4 * PART :, :] = first
    for z in range(many_ref.shape[0]):
        many_ref[z, 12 * PART : 13 * PART, :] = second
        many_ref[z, 13 * PART :, :] = third


def pack(q_rows, copies):
    return pl.pallas_call(
        pack_kernel,
        out_shape=(
            jax.ShapeDtypeStruct((FEW, 128), jnp.bfloat16),
            jax.ShapeDtypeStruct((copies, MANY, 128), jnp.bfloat16),
        ),
        compiler_params=params(8),
        name="pack_queries",
    )(q_rows)


def unpack(few, many, r, zs):
    def gather(get, at, size):
        return [get(z, at, size) for z in range(zs)]

    if r == 0:
        blocks = [
            gather(few, k * PART, PART) + gather(many, 3 * k * PART, PART) for k in range(4)
        ]
        rope = gather(few, 4 * PART, PART) + gather(many, 12 * PART, PART)
    else:
        blocks = [gather(many, (3 * k + 1) * PART, 2 * PART) for k in range(4)]
        rope = gather(many, 12 * PART, 2 * PART)
    latent = jnp.concatenate([jnp.concatenate(block) for block in blocks], axis=1)
    return latent, jnp.concatenate(rope)


def spread(r, zs):
    if r == 0:
        for half in range(2):
            for z in range(zs):
                yield (half * zs + z) * PART, z * 4 * PART + half * PART, PART
    else:
        for z in range(zs):
            yield z * 2 * PART, (z * 4 + 2) * PART, 2 * PART


def beside(rope, r):
    blank = jnp.zeros_like(rope)
    return jnp.concatenate([rope, blank] if r == 0 else [blank, rope], axis=0)


def partial_kernel(place, few_ref, many_ref, keys_ref, bias_ref, out_ref, cols):
    zs = many_ref.shape[0]
    count = zs * 2 * PART
    for r in range(2):
        latent, rope = unpack(
            lambda z, at, size: few_ref[z, place, at : at + size, :],
            lambda z, at, size: many_ref[z, at : at + size, :],
            r,
            zs,
        )
        values = keys_ref[r, :512, :]
        scores = matmul(latent, values) + matmul(rope, beside(keys_ref[r, 512:, :], r))
        bias = bias_ref[r]
        scores = (scores.reshape(count // STEPS, STEPS, -1) + bias[None]).reshape(count, -1)
        top = jnp.maximum(jnp.max(scores, axis=1, keepdims=True) * score_scale, FLOOR)
        top = top.astype(jnp.bfloat16).astype(jnp.float32)
        weights = jnp.exp2(scores * (score_scale * LOG2E) - top * LOG2E)
        total = jnp.sum(weights, axis=1, keepdims=True)
        summed = matmul_t(weights.astype(jnp.bfloat16), values).astype(jnp.bfloat16)
        lanes = iota((count, 128), 1)
        meta = jnp.where(lanes == 0, top, jnp.where(lanes == 1, total, 0.0))
        for come, to, size in spread(r, zs):
            out_ref[to : to + size, :] = summed[come : come + size]
            cols[to : to + size, :] = meta[come : come + size]
    end = zs * 4 * PART
    out_ref[end : end + 16, :] = cols[...].T[:16].astype(jnp.bfloat16)


def local_partial(place, few, many, keys, bias):
    queries = many.shape[0] * 4 * PART
    return pl.pallas_call(
        functools.partial(partial_kernel, place),
        out_shape=jax.ShapeDtypeStruct((queries + 16, 512), jnp.bfloat16),
        scratch_shapes=[pltpu.VMEM((queries, 128), jnp.float32)],
        compiler_params=params(32),
        cost_estimate=pl.CostEstimate(
            flops=2 * queries * keys.shape[2] * 1152,
            bytes_accessed=4 * MIB,
            transcendentals=queries * keys.shape[2],
        ),
        name="local_partial",
    )(few, many, keys, bias)


def combine_kernel(a_ref, b_ref, c_ref, d_ref, out_ref):
    refs = (a_ref, b_ref, c_ref, d_ref)
    zs = out_ref.shape[0]
    chunk = (a_ref.shape[0] - 16) // zs
    count = zs * chunk
    metas = [ref[count : count + 16, :].astype(jnp.float32) for ref in refs]
    tops = [meta[0:1] for meta in metas]
    top = functools.reduce(jnp.maximum, tops)
    factors = [jnp.exp(one - top) for one in tops]
    total = sum(f * meta[1:2] for f, meta in zip(factors, metas))
    place = iota((128, count), 0)
    stacked = jnp.zeros((128, count), jnp.float32)
    for i, f in enumerate(factors):
        stacked = jnp.where(place == i, f, stacked)
    cols = stacked.T
    place = iota((16, count), 0)
    meta = jnp.where(place == 0, top, jnp.where(place == 1, total, 0.0))
    for z in range(zs):
        rows = slice(z * chunk, (z + 1) * chunk)
        merged = sum(
            cols[rows, i : i + 1] * ref[rows, :].astype(jnp.float32) for i, ref in enumerate(refs)
        ).astype(jnp.bfloat16)
        for k in range(4):
            out_ref[z, k * chunk : (k + 1) * chunk, :] = merged[:, k * 128 : (k + 1) * 128]
        tile = meta[:, (z // 2) * 128 : (z // 2 + 1) * 128]
        if z % 2:
            tile = pltpu.roll(tile, 64, 1)
        out_ref[z, 4 * chunk : 4 * chunk + 16, :] = tile.astype(jnp.bfloat16)


def combine(parts, zs, chunk):
    return pl.pallas_call(
        combine_kernel,
        out_shape=jax.ShapeDtypeStruct((zs, 4 * chunk + 16, 128), jnp.bfloat16),
        compiler_params=params(16),
        name="combine_x",
    )(*parts)


def own_kernel(few_ref, many_ref, fresh_ref, bias_ref, sum_ref, meta_ref):
    half = sum_ref.shape[0] // 2
    for r in range(2):
        latent, rope = unpack(
            lambda z, at, size: few_ref[at : at + size, :],
            lambda z, at, size: many_ref[z, at : at + size, :],
            r,
            1,
        )
        fresh = fresh_ref[r]
        scores = matmul_t(latent, fresh[:, :512])
        wide = jnp.concatenate([fresh[:, 512:].astype(jnp.float32)] * 2, axis=1)
        mine = (iota(wide.shape, 1) < 64) == (r == 0)
        scores = scores + matmul_t(rope, jnp.where(mine, wide, 0.0).astype(jnp.bfloat16))
        scores = (scores.reshape(half // STEPS, STEPS, -1) + bias_ref[...][None]).reshape(half, -1)
        top = jnp.max(scores, axis=1, keepdims=True) * score_scale
        weights = jnp.exp2(scores * (score_scale * LOG2E) - top * LOG2E)
        total = jnp.sum(weights, axis=1, keepdims=True)
        at = slice(r * half, (r + 1) * half)
        sum_ref[at, :] = matmul(weights.astype(jnp.bfloat16), fresh[:, :512])
        lanes = iota((half, 128), 1)
        meta_ref[at, :] = jnp.where(lanes == 0, top, jnp.where(lanes == 1, total, 0.0))


def own_part(few, many, fresh, causal):
    count = 4 * PART
    return pl.pallas_call(
        own_kernel,
        grid=(1,),
        in_specs=[
            pl.BlockSpec(few.shape, lambda i: (0, 0)),
            pl.BlockSpec((1, MANY, 128), lambda i: (0, 0, 0)),
            pl.BlockSpec(fresh.shape, lambda i: (0, 0, 0)),
            pl.BlockSpec(causal.shape, lambda i: (0, 0)),
        ],
        out_specs=[
            pl.BlockSpec((count, 512), lambda i: (0, 0)),
            pl.BlockSpec((count, 128), lambda i: (0, 0)),
        ],
        out_shape=(
            jax.ShapeDtypeStruct((count, 512), jnp.float32),
            jax.ShapeDtypeStruct((count, 128), jnp.float32),
        ),
        compiler_params=params(8),
        name="own_part",
    )(few, many, fresh, causal)


def merge_kernel(got_ref, sum_ref, meta_ref, up_ref, out_ref):
    zs = got_ref.shape[0]
    count = sum_ref.shape[0]
    heads = up_ref.shape[0]
    rows = count // (heads * STEPS)
    place = iota((128, 128), 0)
    stacked = jnp.zeros((128, 128), jnp.float32)
    for z in range(zs):
        meta = got_ref[z, 4 * count : 4 * count + 16, :].astype(jnp.float32)
        stacked = jnp.where(place == z, meta[0:1], stacked)
        stacked = jnp.where(place == zs + z, meta[1:2], stacked)
    cols = stacked.T[:count]
    tops, totals = cols[:, :zs], cols[:, zs : 2 * zs]
    own_top, own_total = meta_ref[:, 0:1], meta_ref[:, 1:2]
    top = jnp.maximum(jnp.max(tops, axis=1, keepdims=True), own_top)
    factors = jnp.exp(tops - top)
    own_factor = jnp.exp(own_top - top)
    bottom = jnp.sum(factors * totals, axis=1, keepdims=True) + own_factor * own_total
    pieces = []
    for k in range(4):
        piece = own_factor * sum_ref[:, k * 128 : (k + 1) * 128]
        for z in range(zs):
            block = got_ref[z, k * count : (k + 1) * count, :].astype(jnp.float32)
            piece = piece + factors[:, z : z + 1] * block
        pieces.append(piece / bottom)
    merged = jnp.concatenate(pieces, axis=1)
    for h in range(heads):
        mine = jnp.concatenate(
            [merged[(r * heads + h) * STEPS : (r * heads + h + 1) * STEPS] for r in range(rows)]
        ).astype(jnp.bfloat16)
        lifted = matmul(mine, up_ref[h]).astype(jnp.bfloat16)
        for copy in range(out_ref.shape[0]):
            out_ref[copy, :, h * 128 : (h + 1) * 128] = lifted


def merge(got, own_sum, own_meta, w_uv, copies):
    shape = (copies, own_sum.shape[0] // w_uv.shape[0], w_uv.shape[0] * w_uv.shape[2])
    return pl.pallas_call(
        merge_kernel,
        out_shape=jax.ShapeDtypeStruct(shape, jnp.bfloat16),
        compiler_params=params(16),
        name="merge_up",
    )(got, own_sum, own_meta, w_uv)


def project_kernel(rows_ref, w_ref, out_ref):
    n = rows_ref.shape[0]
    to, come = iota((n, n), 0), iota((n, n), 1)
    rows = n // STEPS
    here = (to % rows) * STEPS + to // rows == come
    here = here.astype(jnp.float32).astype(jnp.bfloat16)
    ordered = matmul(here, rows_ref[...]).astype(jnp.bfloat16)
    out_ref[...] = matmul_t(ordered, w_ref[...]).astype(jnp.bfloat16)


def project(rows, w_out_t):
    return pl.pallas_call(
        project_kernel,
        out_shape=jax.ShapeDtypeStruct((rows.shape[0], w_out_t.shape[0]), jnp.bfloat16),
        compiler_params=params(16),
        name="project_out",
    )(rows, w_out_t)


def shift(value, axis, by, size):
    return lax.ppermute(value, axis, [(i, (i + by) % size) for i in range(size)])


def after(value, earlier):
    return lax.optimization_barrier((value, earlier))[0]


def swap_all(value, axis):
    return lax.all_to_all(value, axis, split_axis=0, concat_axis=0, tiled=True)


def body(latent_cache, queries, new_latent, lengths, selection, w_uv, w_out):
    steps, rows, heads, width = queries.shape
    keys = latent_cache.shape[1]
    shard = lax.axis_index("x") * Z_SIZE + lax.axis_index("z")

    q_rows = jnp.transpose(queries, (1, 2, 0, 3)).reshape(rows * heads * steps, width)
    few, many = pack(q_rows, Z_SIZE)
    line = swap_all(many, "z")
    cross = jnp.stack([few] + [shift(few, "x", d, X_SIZE) for d in range(1, X_SIZE)])
    cross = jnp.broadcast_to(cross[None], (Z_SIZE,) + cross.shape)
    line, cross = lax.optimization_barrier((line, cross))
    cross = swap_all(cross, "z")
    far = shift(line, "x", 2, X_SIZE)
    left = shift(line, "x", 1, X_SIZE)
    right = shift(line, "x", -1, X_SIZE)

    blocks = shard * (keys // BLOCK) + jnp.arange(keys // BLOCK, dtype=jnp.int32)
    chosen = jnp.any(selection[:, :, :, None] == blocks, axis=2)
    positions = shard * keys + jnp.arange(keys, dtype=jnp.int32)
    live = jnp.repeat(chosen, BLOCK, axis=2) & (positions < lengths[:, None])[None]
    bias = jnp.where(jnp.transpose(live, (1, 0, 2)), 0.0, DEAD)
    cache_t = jnp.transpose(latent_cache, (0, 2, 1))

    ids = jnp.arange(128, dtype=jnp.int32)
    causal = jnp.where(ids[None, :] <= jnp.arange(steps)[:, None], 0.0, DEAD)
    fresh = jnp.pad(jnp.transpose(new_latent, (1, 0, 2)), ((0, 0), (0, 128 - steps), (0, 0)))
    own_sum, own_meta = own_part(few, many, fresh, causal)

    here = local_partial(0, cross, line, cache_t, bias)
    for_left = local_partial(1, cross, left, cache_t, bias)
    for_right = local_partial(3, cross, right, cache_t, bias)
    for_far = local_partial(2, cross, after(far, here), cache_t, bias)
    parts = [
        here,
        shift(for_left, "x", -1, X_SIZE),
        shift(for_right, "x", 1, X_SIZE),
        shift(for_far, "x", 2, X_SIZE),
    ]
    got = swap_all(combine(parts, Z_SIZE, rows * heads * steps), "z")
    groups = lax.axis_size(("y", "core"))
    attention = swap_all(merge(got, own_sum, own_meta, w_uv, groups), ("y", "core"))
    shares = project(attention.reshape(groups * rows * steps, -1), w_out.T)
    shares = shares.reshape(X_SIZE * Z_SIZE, -1, shares.shape[1])
    got_shares = swap_all(shares, ("x", "z"))
    return jnp.sum(got_shares.astype(jnp.float32), axis=0).astype(jnp.bfloat16)


def solution(mesh):
    batch = mesh.shape["batch"]
    fine = Mesh(mesh.devices.reshape(X_SIZE, Z_SIZE, batch // 2, 2), ("x", "z", "y", "core"))
    ctx, rows = ("x", "z"), ("y", "core")
    return jax.shard_map(
        body,
        mesh=fine,
        in_specs=(
            P(rows, ctx, None),
            P(None, rows, ctx, None),
            P(None, rows, None),
            P(rows),
            P(None, rows, None),
            P(ctx, None, None),
            P(ctx, rows),
        ),
        out_specs=P(ctx, rows),
        check_vma=False,
    )
```

```python
import functools

import jax
import jax.numpy as jnp
from jax import lax
from jax.experimental import pallas as pl
from jax.experimental.pallas import tpu as pltpu
from jax.sharding import Mesh, PartitionSpec as P

BLOCK = 64
X_SIZE = 4
Z_SIZE = 8
STEPS = 8
LOG2E = 1.4426950408889634
DEAD = -1e30
FLOOR = -1e20
score_scale = 192.0 ** (-0.5)

MIB = 2**20


def params(mib):
    return pltpu.CompilerParams(vmem_limit_bytes=mib * MIB)


def matmul(a, b):
    return jnp.dot(a, b, preferred_element_type=jnp.float32)


def matmul_t(a, b):
    return lax.dot_general(a, b, (((1,), (1,)), ((), ())), preferred_element_type=jnp.float32)


def iota(shape, axis):
    return lax.broadcasted_iota(jnp.int32, shape, axis)


def pack_kernel(q_ref, out_ref):
    count = q_ref.shape[0]
    half = count // 2
    blocks = [q_ref[:, k * 128 : (k + 1) * 128] for k in range(4)]
    rope = q_ref[:, 512:576].astype(jnp.float32)
    wide = jnp.concatenate([rope, rope], axis=1)
    rope = jnp.where(iota((half, 128), 1) < 64, wide[:half], wide[half:]).astype(jnp.bfloat16)
    for z in range(out_ref.shape[0]):
        for k in range(4):
            out_ref[z, k * count : (k + 1) * count, :] = blocks[k]
        out_ref[z, 4 * count :, :] = rope


def pack(q_rows, copies):
    count = q_rows.shape[0]
    return pl.pallas_call(
        pack_kernel,
        out_shape=jax.ShapeDtypeStruct((copies, 4 * count + count // 2, 128), jnp.bfloat16),
        compiler_params=params(8),
        name="pack_queries",
    )(q_rows)


def unpack(refs, r):
    length = refs[0].shape[1]
    count = length * 2 // 9
    half = count // 2
    blocks = []
    for k in range(4):
        at = slice(k * count + r * half, k * count + (r + 1) * half)
        blocks.append(jnp.concatenate([ref[z, at, :] for ref in refs for z in range(ref.shape[0])]))
    latent = jnp.concatenate(blocks, axis=1)
    at = slice(4 * count, 4 * count + half)
    rope = jnp.concatenate([ref[z, at, :] for ref in refs for z in range(ref.shape[0])])
    return latent, rope


def beside(rope, r):
    blank = jnp.zeros_like(rope)
    return jnp.concatenate([rope, blank] if r == 0 else [blank, rope], axis=0)


def cut_for_z(meta, z):
    tile = meta[:, (z // 2) * 128 : (z // 2 + 1) * 128]
    if z % 2:
        tile = pltpu.roll(tile, 64, 1)
    return tile[:16].astype(jnp.bfloat16)


def partial_kernel(for_z, q_ref, keys_ref, bias_ref, out_ref, cols):
    q_refs = [q_ref]
    zs = q_ref.shape[0]
    chunk = q_ref.shape[1] * 2 // 9
    half = chunk // 2
    count = zs * half
    for r in range(2):
        latent, rope = unpack(q_refs, r)
        values = keys_ref[r, :512, :]
        scores = matmul(latent, values) + matmul(rope, beside(keys_ref[r, 512:, :], r))
        bias = bias_ref[r]
        scores = (scores.reshape(count // STEPS, STEPS, -1) + bias[None]).reshape(count, -1)
        top = jnp.maximum(jnp.max(scores, axis=1, keepdims=True) * score_scale, FLOOR)
        top = top.astype(jnp.bfloat16).astype(jnp.float32)
        weights = jnp.exp2(scores * (score_scale * LOG2E) - top * LOG2E)
        total = jnp.sum(weights, axis=1, keepdims=True)
        summed = matmul_t(weights.astype(jnp.bfloat16), values).astype(jnp.bfloat16)
        lanes = iota((count, 128), 1)
        meta = jnp.where(lanes == 0, top, jnp.where(lanes == 1, total, 0.0))
        for z in range(zs):
            at = z * chunk + r * half
            part = slice(z * half, (z + 1) * half)
            cols[at : at + half, :] = meta[part]
            if not for_z:
                out_ref[at : at + half, :] = summed[part]
                continue
            for k in range(4):
                to = k * chunk + r * half
                out_ref[z, to : to + half, :] = summed[part, k * 128 : (k + 1) * 128]
    meta = cols[...].T
    if for_z:
        for z in range(zs):
            out_ref[z, 4 * chunk :, :] = cut_for_z(meta, z)
    else:
        out_ref[zs * chunk :, :] = meta[:16].astype(jnp.bfloat16)


def local_partial(q_chunk, keys, bias, for_z=False):
    zs, chunk = q_chunk.shape[0], q_chunk.shape[1] * 2 // 9
    queries = zs * chunk
    shape = (zs, 4 * chunk + 16, 128) if for_z else (queries + 16, 512)
    return pl.pallas_call(
        functools.partial(partial_kernel, for_z),
        out_shape=jax.ShapeDtypeStruct(shape, jnp.bfloat16),
        scratch_shapes=[pltpu.VMEM((queries, 128), jnp.float32)],
        compiler_params=params(32),
        cost_estimate=pl.CostEstimate(
            flops=2 * queries * keys.shape[2] * 1152,
            bytes_accessed=4 * MIB,
            transcendentals=queries * keys.shape[2],
        ),
        name="local_partial",
    )(q_chunk, keys, bias)


def combine_kernel(*refs):
    refs, out_ref = refs[:-1], refs[-1]
    zs = out_ref.shape[0]
    chunk = (refs[0].shape[0] - 16) // zs
    count = zs * chunk
    metas = [ref[count : count + 16, :].astype(jnp.float32) for ref in refs]
    tops = [meta[0:1] for meta in metas]
    top = functools.reduce(jnp.maximum, tops)
    factors = [jnp.exp(one - top) for one in tops]
    total = sum(f * meta[1:2] for f, meta in zip(factors, metas))
    place = iota((128, count), 0)
    stacked = jnp.zeros((128, count), jnp.float32)
    for i, f in enumerate(factors):
        stacked = jnp.where(place == i, f, stacked)
    cols = stacked.T
    place = iota((16, count), 0)
    meta = jnp.where(place == 0, top, jnp.where(place == 1, total, 0.0))
    for z in range(zs):
        rows = slice(z * chunk, (z + 1) * chunk)
        merged = sum(
            cols[rows, i : i + 1] * ref[rows, :].astype(jnp.float32) for i, ref in enumerate(refs)
        ).astype(jnp.bfloat16)
        for k in range(4):
            out_ref[z, k * chunk : (k + 1) * chunk, :] = merged[:, k * 128 : (k + 1) * 128]
        out_ref[z, 4 * chunk :, :] = cut_for_z(meta, z)


def combine(parts, zs, chunk):
    return pl.pallas_call(
        combine_kernel,
        out_shape=jax.ShapeDtypeStruct((zs, 4 * chunk + 16, 128), jnp.bfloat16),
        compiler_params=params(16),
        name="combine_x",
    )(*parts)


def own_kernel(q_ref, fresh_ref, bias_ref, sum_ref, meta_ref):
    half = sum_ref.shape[0] // 2
    for r in range(2):
        latent, rope = unpack([q_ref], r)
        fresh = fresh_ref[r]
        scores = matmul_t(latent, fresh[:, :512])
        wide = jnp.concatenate([fresh[:, 512:].astype(jnp.float32)] * 2, axis=1)
        mine = (iota(wide.shape, 1) < 64) == (r == 0)
        scores = scores + matmul_t(rope, jnp.where(mine, wide, 0.0).astype(jnp.bfloat16))
        scores = (scores.reshape(half // STEPS, STEPS, -1) + bias_ref[...][None]).reshape(half, -1)
        top = jnp.max(scores, axis=1, keepdims=True) * score_scale
        weights = jnp.exp2(scores * (score_scale * LOG2E) - top * LOG2E)
        total = jnp.sum(weights, axis=1, keepdims=True)
        at = slice(r * half, (r + 1) * half)
        sum_ref[at, :] = matmul(weights.astype(jnp.bfloat16), fresh[:, :512])
        lanes = iota((half, 128), 1)
        meta_ref[at, :] = jnp.where(lanes == 0, top, jnp.where(lanes == 1, total, 0.0))


def own_part(packed, fresh, causal):
    length = packed.shape[1]
    count = length * 2 // 9
    return pl.pallas_call(
        own_kernel,
        grid=(1,),
        in_specs=[
            pl.BlockSpec((1, length, 128), lambda i: (0, 0, 0)),
            pl.BlockSpec(fresh.shape, lambda i: (0, 0, 0)),
            pl.BlockSpec(causal.shape, lambda i: (0, 0)),
        ],
        out_specs=[
            pl.BlockSpec((count, 512), lambda i: (0, 0)),
            pl.BlockSpec((count, 128), lambda i: (0, 0)),
        ],
        out_shape=(
            jax.ShapeDtypeStruct((count, 512), jnp.float32),
            jax.ShapeDtypeStruct((count, 128), jnp.float32),
        ),
        compiler_params=params(8),
        name="own_part",
    )(packed, fresh, causal)


def columns(got, count):
    place = iota((128, 128), 0)
    stacked = jnp.zeros((128, 128), jnp.float32)
    for i, read in enumerate(got):
        meta = read(4 * count, 16).astype(jnp.float32)
        stacked = jnp.where(place == i, meta[0:1], stacked)
        stacked = jnp.where(place == len(got) + i, meta[1:2], stacked)
    cols = stacked.T[:count]
    return cols[:, : len(got)], cols[:, len(got) : 2 * len(got)]


def scaled(got, factors, count, k):
    return sum(
        factors[:, i : i + 1] * read(k * count, count).astype(jnp.float32)
        for i, read in enumerate(got)
    )


def reader(ref, z=None):
    if z is None:
        return lambda at, size: ref[at : at + size, :]
    return lambda at, size: ref[z, at : at + size, :]


def gather_kernel(got_ref, out_ref):
    count = (got_ref.shape[1] - 16) // 4
    got = [reader(got_ref, z) for z in range(got_ref.shape[0])]
    tops, totals = columns(got, count)
    top = jnp.max(tops, axis=1, keepdims=True)
    factors = jnp.exp(tops - top)
    total = jnp.sum(factors * totals, axis=1, keepdims=True)
    for k in range(4):
        out_ref[k * count : (k + 1) * count, :] = scaled(got, factors, count, k).astype(
            jnp.bfloat16
        )
    lanes = iota((count, 128), 1)
    meta = jnp.where(lanes == 0, top, jnp.where(lanes == 1, total, 0.0))
    meta = jnp.concatenate([meta, jnp.zeros((128 - count, 128), jnp.float32)])
    out_ref[4 * count :, :] = meta.T[:16].astype(jnp.bfloat16)


def combine_over_z(got):
    return pl.pallas_call(
        gather_kernel,
        out_shape=jax.ShapeDtypeStruct(got.shape[1:], jnp.bfloat16),
        compiler_params=params(16),
        name="combine_z",
    )(got)


def merge_kernel(got_ref, far_ref, sum_ref, meta_ref, up_ref, out_ref):
    count = sum_ref.shape[0]
    heads = up_ref.shape[0]
    rows = count // (heads * STEPS)
    got = [reader(got_ref, z) for z in range(got_ref.shape[0])] + [reader(far_ref)]
    tops, totals = columns(got, count)
    own_top, own_total = meta_ref[:, 0:1], meta_ref[:, 1:2]
    top = jnp.maximum(jnp.max(tops, axis=1, keepdims=True), own_top)
    factors = jnp.exp(tops - top)
    own_factor = jnp.exp(own_top - top)
    bottom = jnp.sum(factors * totals, axis=1, keepdims=True) + own_factor * own_total
    pieces = []
    for k in range(4):
        piece = own_factor * sum_ref[:, k * 128 : (k + 1) * 128]
        pieces.append((piece + scaled(got, factors, count, k)) / bottom)
    merged = jnp.concatenate(pieces, axis=1)
    for h in range(heads):
        mine = jnp.concatenate(
            [merged[(r * heads + h) * STEPS : (r * heads + h + 1) * STEPS] for r in range(rows)]
        ).astype(jnp.bfloat16)
        lifted = matmul(mine, up_ref[h]).astype(jnp.bfloat16)
        for copy in range(out_ref.shape[0]):
            out_ref[copy, :, h * 128 : (h + 1) * 128] = lifted


def merge(got, far, own_sum, own_meta, w_uv, copies):
    shape = (copies, own_sum.shape[0] // w_uv.shape[0], w_uv.shape[0] * w_uv.shape[2])
    return pl.pallas_call(
        merge_kernel,
        out_shape=jax.ShapeDtypeStruct(shape, jnp.bfloat16),
        compiler_params=params(16),
        name="merge_up",
    )(got, far, own_sum, own_meta, w_uv)


def project_kernel(rows_ref, w_ref, out_ref):
    n = rows_ref.shape[0]
    to, come = iota((n, n), 0), iota((n, n), 1)
    rows = n // STEPS
    here = (to % rows) * STEPS + to // rows == come
    here = here.astype(jnp.float32).astype(jnp.bfloat16)
    ordered = matmul(here, rows_ref[...]).astype(jnp.bfloat16)
    out_ref[...] = matmul_t(ordered, w_ref[...]).astype(jnp.bfloat16)


def project(rows, w_out_t):
    return pl.pallas_call(
        project_kernel,
        out_shape=jax.ShapeDtypeStruct((rows.shape[0], w_out_t.shape[0]), jnp.bfloat16),
        compiler_params=params(16),
        name="project_out",
    )(rows, w_out_t)


def shift(value, axis, by, size):
    return lax.ppermute(value, axis, [(i, (i + by) % size) for i in range(size)])


def after(value, earlier):
    return lax.optimization_barrier((value, earlier))[0]


def swap_all(value, axis):
    return lax.all_to_all(value, axis, split_axis=0, concat_axis=0, tiled=True)


def body(latent_cache, queries, new_latent, lengths, selection, w_uv, w_out):
    steps, rows, heads, width = queries.shape
    keys = latent_cache.shape[1]
    shard = lax.axis_index("x") * Z_SIZE + lax.axis_index("z")

    q_rows = jnp.transpose(queries, (1, 2, 0, 3)).reshape(rows * heads * steps, width)
    packed = pack(q_rows, Z_SIZE)
    line = swap_all(packed, "z")
    far = shift(packed[0], "x", 2, X_SIZE)
    far = swap_all(jnp.broadcast_to(far[None], packed.shape), "z")
    left = shift(line, "x", 1, X_SIZE)
    right = shift(line, "x", -1, X_SIZE)

    blocks = shard * (keys // BLOCK) + jnp.arange(keys // BLOCK, dtype=jnp.int32)
    chosen = jnp.any(selection[:, :, :, None] == blocks, axis=2)
    positions = shard * keys + jnp.arange(keys, dtype=jnp.int32)
    live = jnp.repeat(chosen, BLOCK, axis=2) & (positions < lengths[:, None])[None]
    bias = jnp.where(jnp.transpose(live, (1, 0, 2)), 0.0, DEAD)
    cache_t = jnp.transpose(latent_cache, (0, 2, 1))

    ids = jnp.arange(128, dtype=jnp.int32)
    causal = jnp.where(ids[None, :] <= jnp.arange(steps)[:, None], 0.0, DEAD)
    fresh = jnp.pad(jnp.transpose(new_latent, (1, 0, 2)), ((0, 0), (0, 128 - steps), (0, 0)))
    own_sum, own_meta = own_part(packed, fresh, causal)

    here = local_partial(line, cache_t, bias)
    for_left = local_partial(left, cache_t, bias)
    for_right = local_partial(right, cache_t, bias)
    for_far = local_partial(after(far, here), cache_t, bias, for_z=True)
    parts = [
        here,
        shift(for_left, "x", -1, X_SIZE),
        shift(for_right, "x", 1, X_SIZE),
    ]
    home = shift(combine_over_z(swap_all(for_far, "z")), "x", 2, X_SIZE)
    got = swap_all(combine(parts, Z_SIZE, rows * heads * steps), "z")
    groups = lax.axis_size(("y", "core"))
    attention = swap_all(merge(got, home, own_sum, own_meta, w_uv, groups), ("y", "core"))
    shares = project(attention.reshape(groups * rows * steps, -1), w_out.T)
    shares = shares.reshape(X_SIZE * Z_SIZE, -1, shares.shape[1])
    got_shares = swap_all(shares, ("x", "z"))
    return jnp.sum(got_shares.astype(jnp.float32), axis=0).astype(jnp.bfloat16)


def solution(mesh):
    batch = mesh.shape["batch"]
    fine = Mesh(mesh.devices.reshape(X_SIZE, Z_SIZE, batch // 2, 2), ("x", "z", "y", "core"))
    ctx, rows = ("x", "z"), ("y", "core")
    return jax.shard_map(
        body,
        mesh=fine,
        in_specs=(
            P(rows, ctx, None),
            P(None, rows, ctx, None),
            P(None, rows, None),
            P(rows),
            P(None, rows, None),
            P(ctx, None, None),
            P(ctx, rows),
        ),
        out_specs=P(ctx, rows),
        check_vma=False,
    )
```

```python
import functools

import jax
import jax.numpy as jnp
from jax import lax
from jax.experimental import pallas as pl
from jax.experimental.pallas import tpu as pltpu
from jax.sharding import Mesh, PartitionSpec as P

BLOCK = 64
X_SIZE = 4
Z_SIZE = 8
STEPS = 8
LOG2E = 1.4426950408889634
DEAD = -1e30
FLOOR = -1e20
score_scale = 192.0 ** (-0.5)

MIB = 2**20


def params(mib):
    return pltpu.CompilerParams(vmem_limit_bytes=mib * MIB)


def matmul(a, b):
    return jnp.dot(a, b, preferred_element_type=jnp.float32)


def matmul_t(a, b):
    return lax.dot_general(a, b, (((1,), (1,)), ((), ())), preferred_element_type=jnp.float32)


def iota(shape, axis):
    return lax.broadcasted_iota(jnp.int32, shape, axis)


def pack_kernel(q_ref, out_ref, packed, sems):
    count = q_ref.shape[0]
    half = count // 2
    blocks = [q_ref[:, k * 128 : (k + 1) * 128] for k in range(4)]
    rope = q_ref[:, 512:576].astype(jnp.float32)
    wide = jnp.concatenate([rope, rope], axis=1)
    rope = jnp.where(iota((half, 128), 1) < 64, wide[:half], wide[half:]).astype(jnp.bfloat16)
    for k in range(4):
        packed[k * count : (k + 1) * count, :] = blocks[k]
    packed[4 * count :, :] = rope
    copies = [
        pltpu.make_async_copy(packed, out_ref.at[z], sems.at[z]) for z in range(out_ref.shape[0])
    ]
    for copy in copies:
        copy.start()
    for copy in copies:
        copy.wait()


def pack(q_rows, copies):
    count = q_rows.shape[0]
    return pl.pallas_call(
        pack_kernel,
        out_shape=jax.ShapeDtypeStruct((copies, 4 * count + count // 2, 128), jnp.bfloat16),
        out_specs=pl.BlockSpec(memory_space=pl.ANY),
        scratch_shapes=[
            pltpu.VMEM((4 * count + count // 2, 128), jnp.bfloat16),
            pltpu.SemaphoreType.DMA((copies,)),
        ],
        compiler_params=params(8),
        name="pack_queries",
    )(q_rows)


def unpack(refs, r):
    length = refs[0].shape[1]
    count = length * 2 // 9
    half = count // 2
    blocks = []
    for k in range(4):
        at = slice(k * count + r * half, k * count + (r + 1) * half)
        blocks.append(jnp.concatenate([ref[z, at, :] for ref in refs for z in range(ref.shape[0])]))
    latent = jnp.concatenate(blocks, axis=1)
    at = slice(4 * count, 4 * count + half)
    rope = jnp.concatenate([ref[z, at, :] for ref in refs for z in range(ref.shape[0])])
    return latent, rope


def beside(rope, r):
    blank = jnp.zeros_like(rope)
    return jnp.concatenate([rope, blank] if r == 0 else [blank, rope], axis=0)


def partial_kernel(*refs):
    q_refs, (keys_ref, bias_ref, out_ref, cols) = refs[:-4], refs[-4:]
    zs = sum(ref.shape[0] for ref in q_refs)
    chunk = q_refs[0].shape[1] * 2 // 9
    half = chunk // 2
    count = zs * half
    for r in range(2):
        latent, rope = unpack(q_refs, r)
        values = keys_ref[r, :512, :]
        scores = matmul(latent, values) + matmul(rope, beside(keys_ref[r, 512:, :], r))
        bias = bias_ref[r]
        scores = (scores.reshape(count // STEPS, STEPS, -1) + bias[None]).reshape(count, -1)
        top = jnp.maximum(jnp.max(scores, axis=1, keepdims=True) * score_scale, FLOOR)
        top = top.astype(jnp.bfloat16).astype(jnp.float32)
        weights = jnp.exp2(scores * (score_scale * LOG2E) - top * LOG2E)
        total = jnp.sum(weights, axis=1, keepdims=True)
        summed = matmul_t(weights.astype(jnp.bfloat16), values).astype(jnp.bfloat16)
        lanes = iota((count, 128), 1)
        meta = jnp.where(lanes == 0, top, jnp.where(lanes == 1, total, 0.0))
        for z in range(zs):
            at = z * chunk + r * half
            part = slice(z * half, (z + 1) * half)
            out_ref[at : at + half, :] = summed[part]
            cols[at : at + half, :] = meta[part]
    end = zs * chunk
    out_ref[end : end + 16, :] = cols[...].T[:16].astype(jnp.bfloat16)


def local_partial(q_chunks, keys, bias):
    chunk = q_chunks[0].shape[1] * 2 // 9
    queries = sum(q.shape[0] for q in q_chunks) * chunk
    return pl.pallas_call(
        partial_kernel,
        out_shape=jax.ShapeDtypeStruct((queries + 16, 512), jnp.bfloat16),
        scratch_shapes=[pltpu.VMEM((queries, 128), jnp.float32)],
        compiler_params=params(32),
        cost_estimate=pl.CostEstimate(
            flops=2 * queries * keys.shape[2] * 1152,
            bytes_accessed=4 * MIB,
            transcendentals=queries * keys.shape[2],
        ),
        name="local_partial",
    )(*q_chunks, keys, bias)


def combine_kernel(a_ref, b_ref, c_ref, d_ref, out_ref, pieces, sems):
    refs = (a_ref, b_ref, c_ref, d_ref)
    zs = out_ref.shape[0]
    chunk = (a_ref.shape[0] - 16) // zs
    count = zs * chunk
    metas = [ref[count : count + 16, :].astype(jnp.float32) for ref in refs]
    tops = [meta[0:1] for meta in metas]
    top = functools.reduce(jnp.maximum, tops)
    factors = [jnp.exp(one - top) for one in tops]
    total = sum(f * meta[1:2] for f, meta in zip(factors, metas))
    place = iota((128, count), 0)
    stacked = jnp.zeros((128, count), jnp.float32)
    for i, f in enumerate(factors):
        stacked = jnp.where(place == i, f, stacked)
    cols = stacked.T
    place = iota((16, count), 0)
    meta = jnp.where(place == 0, top, jnp.where(place == 1, total, 0.0))
    copies = [pltpu.make_async_copy(pieces.at[z], out_ref.at[z], sems.at[z]) for z in range(zs)]
    for z in range(zs):
        rows = slice(z * chunk, (z + 1) * chunk)
        merged = sum(
            cols[rows, i : i + 1] * ref[rows, :].astype(jnp.float32) for i, ref in enumerate(refs)
        ).astype(jnp.bfloat16)
        for k in range(4):
            pieces[z, k * chunk : (k + 1) * chunk, :] = merged[:, k * 128 : (k + 1) * 128]
        tile = meta[:, (z // 2) * 128 : (z // 2 + 1) * 128]
        if z % 2:
            tile = pltpu.roll(tile, 64, 1)
        pieces[z, 4 * chunk : 4 * chunk + 16, :] = tile.astype(jnp.bfloat16)
        copies[z].start()
    for copy in copies:
        copy.wait()


def combine(parts, zs, chunk):
    return pl.pallas_call(
        combine_kernel,
        out_shape=jax.ShapeDtypeStruct((zs, 4 * chunk + 16, 128), jnp.bfloat16),
        out_specs=pl.BlockSpec(memory_space=pl.ANY),
        scratch_shapes=[
            pltpu.VMEM((zs, 4 * chunk + 16, 128), jnp.bfloat16),
            pltpu.SemaphoreType.DMA((zs,)),
        ],
        compiler_params=params(16),
        name="combine_x",
    )(*parts)


def own_kernel(q_ref, fresh_ref, bias_ref, sum_ref, meta_ref):
    half = sum_ref.shape[0] // 2
    for r in range(2):
        latent, rope = unpack([q_ref], r)
        fresh = fresh_ref[r]
        scores = matmul_t(latent, fresh[:, :512])
        wide = jnp.concatenate([fresh[:, 512:].astype(jnp.float32)] * 2, axis=1)
        mine = (iota(wide.shape, 1) < 64) == (r == 0)
        scores = scores + matmul_t(rope, jnp.where(mine, wide, 0.0).astype(jnp.bfloat16))
        scores = (scores.reshape(half // STEPS, STEPS, -1) + bias_ref[...][None]).reshape(half, -1)
        top = jnp.max(scores, axis=1, keepdims=True) * score_scale
        weights = jnp.exp2(scores * (score_scale * LOG2E) - top * LOG2E)
        total = jnp.sum(weights, axis=1, keepdims=True)
        at = slice(r * half, (r + 1) * half)
        sum_ref[at, :] = matmul(weights.astype(jnp.bfloat16), fresh[:, :512])
        lanes = iota((half, 128), 1)
        meta_ref[at, :] = jnp.where(lanes == 0, top, jnp.where(lanes == 1, total, 0.0))


def own_part(packed, fresh, causal):
    length = packed.shape[1]
    count = length * 2 // 9
    return pl.pallas_call(
        own_kernel,
        grid=(1,),
        in_specs=[
            pl.BlockSpec((1, length, 128), lambda i: (0, 0, 0)),
            pl.BlockSpec(fresh.shape, lambda i: (0, 0, 0)),
            pl.BlockSpec(causal.shape, lambda i: (0, 0)),
        ],
        out_specs=[
            pl.BlockSpec((count, 512), lambda i: (0, 0)),
            pl.BlockSpec((count, 128), lambda i: (0, 0)),
        ],
        out_shape=(
            jax.ShapeDtypeStruct((count, 512), jnp.float32),
            jax.ShapeDtypeStruct((count, 128), jnp.float32),
        ),
        compiler_params=params(8),
        name="own_part",
    )(packed, fresh, causal)


def merge_kernel(got_ref, sum_ref, meta_ref, up_ref, out_ref):
    zs = got_ref.shape[0]
    count = sum_ref.shape[0]
    heads = up_ref.shape[0]
    rows = count // (heads * STEPS)
    place = iota((128, 128), 0)
    stacked = jnp.zeros((128, 128), jnp.float32)
    for z in range(zs):
        meta = got_ref[z, 4 * count : 4 * count + 16, :].astype(jnp.float32)
        stacked = jnp.where(place == z, meta[0:1], stacked)
        stacked = jnp.where(place == zs + z, meta[1:2], stacked)
    cols = stacked.T[:count]
    tops, totals = cols[:, :zs], cols[:, zs : 2 * zs]
    own_top, own_total = meta_ref[:, 0:1], meta_ref[:, 1:2]
    top = jnp.maximum(jnp.max(tops, axis=1, keepdims=True), own_top)
    factors = jnp.exp(tops - top)
    own_factor = jnp.exp(own_top - top)
    bottom = jnp.sum(factors * totals, axis=1, keepdims=True) + own_factor * own_total
    pieces = []
    for k in range(4):
        piece = own_factor * sum_ref[:, k * 128 : (k + 1) * 128]
        for z in range(zs):
            block = got_ref[z, k * count : (k + 1) * count, :].astype(jnp.float32)
            piece = piece + factors[:, z : z + 1] * block
        pieces.append(piece / bottom)
    merged = jnp.concatenate(pieces, axis=1)
    for h in range(heads):
        mine = jnp.concatenate(
            [merged[(r * heads + h) * STEPS : (r * heads + h + 1) * STEPS] for r in range(rows)]
        ).astype(jnp.bfloat16)
        lifted = matmul(mine, up_ref[h]).astype(jnp.bfloat16)
        for copy in range(out_ref.shape[0]):
            out_ref[copy, :, h * 128 : (h + 1) * 128] = lifted


def merge(got, own_sum, own_meta, w_uv, copies):
    shape = (copies, own_sum.shape[0] // w_uv.shape[0], w_uv.shape[0] * w_uv.shape[2])
    return pl.pallas_call(
        merge_kernel,
        out_shape=jax.ShapeDtypeStruct(shape, jnp.bfloat16),
        compiler_params=params(16),
        name="merge_up",
    )(got, own_sum, own_meta, w_uv)


def project_kernel(rows_ref, w_ref, out_ref):
    n = rows_ref.shape[0]
    to, come = iota((n, n), 0), iota((n, n), 1)
    rows = n // STEPS
    here = (to % rows) * STEPS + to // rows == come
    here = here.astype(jnp.float32).astype(jnp.bfloat16)
    ordered = matmul(here, rows_ref[...]).astype(jnp.bfloat16)
    out_ref[...] = matmul_t(ordered, w_ref[...]).astype(jnp.bfloat16)


def project(rows, w_out_t):
    return pl.pallas_call(
        project_kernel,
        out_shape=jax.ShapeDtypeStruct((rows.shape[0], w_out_t.shape[0]), jnp.bfloat16),
        compiler_params=params(16),
        name="project_out",
    )(rows, w_out_t)


def shift(value, axis, by, size):
    return lax.ppermute(value, axis, [(i, (i + by) % size) for i in range(size)])


def after(value, earlier):
    return lax.optimization_barrier((value, earlier))[0]


def swap_all(value, axis):
    return lax.all_to_all(value, axis, split_axis=0, concat_axis=0, tiled=True)


def body(latent_cache, queries, new_latent, lengths, selection, w_uv, w_out):
    steps, rows, heads, width = queries.shape
    keys = latent_cache.shape[1]
    shard = lax.axis_index("x") * Z_SIZE + lax.axis_index("z")

    q_rows = jnp.transpose(queries, (1, 2, 0, 3)).reshape(rows * heads * steps, width)
    packed = pack(q_rows, Z_SIZE)

    selection, lengths = after((selection, lengths), packed)
    blocks = shard * (keys // BLOCK) + jnp.arange(keys // BLOCK, dtype=jnp.int32)
    chosen = jnp.any(selection[:, :, :, None] == blocks, axis=2)
    positions = shard * keys + jnp.arange(keys, dtype=jnp.int32)
    live = jnp.repeat(chosen, BLOCK, axis=2) & (positions < lengths[:, None])[None]
    bias = jnp.where(jnp.transpose(live, (1, 0, 2)), 0.0, DEAD)
    line = after(swap_all(packed, "z"), bias)
    far = shift(line, "x", 2, X_SIZE)
    left = shift(line, "x", 1, X_SIZE)
    right = shift(line, "x", -1, X_SIZE)

    cache_t = jnp.transpose(latent_cache, (0, 2, 1))

    ids = jnp.arange(128, dtype=jnp.int32)
    causal = jnp.where(ids[None, :] <= jnp.arange(steps)[:, None], 0.0, DEAD)
    fresh = jnp.pad(jnp.transpose(new_latent, (1, 0, 2)), ((0, 0), (0, 128 - steps), (0, 0)))
    own_sum, own_meta = own_part(packed, fresh, causal)

    here = local_partial([line], cache_t, bias)
    for_left = local_partial([after(left, here)], cache_t, bias)
    for_right = local_partial([right], cache_t, bias)
    for_far = local_partial([far], cache_t, bias)
    parts = [
        here,
        shift(for_left, "x", -1, X_SIZE),
        shift(for_right, "x", 1, X_SIZE),
        shift(for_far, "x", 2, X_SIZE),
    ]
    got = swap_all(combine(parts, Z_SIZE, rows * heads * steps), "z")
    groups = lax.axis_size(("y", "core"))
    attention = swap_all(merge(got, own_sum, own_meta, w_uv, groups), ("y", "core"))
    shares = project(attention.reshape(groups * rows * steps, -1), w_out.T)
    shares = shares.reshape(X_SIZE * Z_SIZE, -1, shares.shape[1])
    got_shares = swap_all(shares, ("x", "z"))
    return jnp.sum(got_shares.astype(jnp.float32), axis=0).astype(jnp.bfloat16)


def solution(mesh):
    batch = mesh.shape["batch"]
    fine = Mesh(mesh.devices.reshape(X_SIZE, Z_SIZE, batch // 2, 2), ("x", "z", "y", "core"))
    ctx, rows = ("x", "z"), ("y", "core")
    return jax.shard_map(
        body,
        mesh=fine,
        in_specs=(
            P(rows, ctx, None),
            P(None, rows, ctx, None),
            P(None, rows, None),
            P(rows),
            P(None, rows, None),
            P(ctx, None, None),
            P(ctx, rows),
        ),
        out_specs=P(ctx, rows),
        check_vma=False,
    )
```
